768 devices in a mesh: dp: 192 (over x, y_lo, z, core), mp: 4 (over y_hi).
Axes of the slice: x: 4, y: 8 (y_hi: 4, y_lo: 2; y = y_hi * 2 + y_lo), z: 12, core: 2. Of those that a mesh axis runs over, the one named last changes fastest.
Arguments:
- activations: bfloat16 [512, 9216], P('mp', 'dp'), may hold values from -6 to 6
- block_values: bfloat16 [384, 20, 128, 128], P('dp'), may hold values from -0.125 to 0.125
- block_rows: int32 [384, 20], P('dp'), may hold values from 0 to 71, all different within a row
- cotangent: bfloat16 [512, 49152], P('mp', 'dp'), may hold values from -6 to 6
Outputs:
- gelu_out: bfloat16 [512, 49152], P('mp', 'dp')
- input_grad: bfloat16 [512, 9216], P('mp', 'dp')
- block_grad: float32 [384, 20, 128, 128], P('dp', 'mp')
The draws below stay inside these ranges and needn't reach their ends.
Inputs may be any that keep to these rules, and one draw needn't show every extreme that they name: `block_rows`: the 20 entries of each column block are different block rows; every block row is named somewhere.
All inputs are finite; a program needn't handle non-finite values.
Results may differ from the reference program's by a relative error of at most 0.0049.
Values may be sent and summed in bfloat16 or wider, within the bound.
A program may use at most 64 MiB of HBM per device.

```python
import jax
import jax.numpy as jnp
from jax import lax

D = 9216
FF = 49152
BLK = 128
KB = 20
TOKENS = 512
RB = 72
NCB = 384


def level_of(rng, dims, cuts, low, top_value):
    loudness = 1.0
    for dim, blocks in cuts:
        heights = jax.random.uniform(jax.random.fold_in(jax.random.fold_in(rng, 6), dim), (blocks,), jnp.float32, low / len(cuts), top_value / len(cuts))
        loudness = loudness * jnp.repeat(jnp.exp(heights), dims[dim] // blocks).reshape((-1,) + (1,) * (len(dims) - 1 - dim))
    return loudness


def distinct(key, rows, amount, top, lift):
    sequence = jax.random.permutation(jax.random.fold_in(key, 1), amount)
    pull = sequence
    for power in range(3):
        pull = pull * pull // amount
    pull = pull * lift // amount
    lots = jax.random.randint(jax.random.fold_in(key, 2), (rows, amount), 0, 4096) + pull
    holders = jax.random.permutation(jax.random.fold_in(key, 3), rows)[jnp.arange(amount) % rows]
    lots = jnp.where(jnp.arange(rows)[:, None] == holders[None, :], 1 << 14, lots)
    merit = lots * amount + jnp.arange(amount)
    return lax.top_k(merit.astype(jnp.int32), top)[1].astype(jnp.int32)


def scatter_about(stream_key, shape, width, bound, cuts=(), dtype=jnp.bfloat16):
    result = width * jax.random.normal(stream_key, shape, jnp.float32)
    if cuts:
        result = result * level_of(stream_key, shape, cuts, -0.22, 0.18)
    return jnp.clip(result, -bound, bound).astype(dtype)


def setup_inputs(seed: int = 0) -> dict:
    seeds = jax.random.split(jax.random.key(seed), 5)
    return {
        "activations": scatter_about(seeds[0], (TOKENS, D), 1.0, 6.0, ((0, 4), (1, 192))),
        "block_values": scatter_about(seeds[1], (NCB, KB, BLK, BLK), (KB * BLK) ** -0.5, 0.125, ((0, 192),)),
        "block_rows": distinct(seeds[2], NCB, RB, KB, 2275),
        "cotangent": scatter_about(seeds[3], (TOKENS, FF), 1.0, 6.0, ((0, 4), (1, 192))),
    }


def gelu_tanh(values):
    return jax.nn.gelu(values, approximate=True)

def reference(activations, block_values, block_rows, cotangent):
    num_tokens = activations.shape[0]
    x_blocks = activations.reshape(num_tokens, RB, BLK)
    cot_columns = jnp.transpose(cotangent.reshape(num_tokens, NCB, BLK), (1, 0, 2))

    def column(running, column_data):
        w_column, row_list, cot_column = column_data
        picked_rows = jnp.take(x_blocks, row_list, axis=1).astype(jnp.float32)
        weights32 = w_column.astype(jnp.float32)
        pre_act = jnp.einsum('tki,kij->tj', picked_rows, weights32, precision=lax.Precision.HIGHEST)
        activated = gelu_tanh(pre_act).astype(jnp.bfloat16)
        unused, pull_back = jax.vjp(gelu_tanh, pre_act)
        slopes = pull_back(cot_column.astype(jnp.float32))[0].astype(jnp.bfloat16)
        slopes32 = slopes.astype(jnp.float32)
        contrib = jnp.einsum('tj,kij->tki', slopes32, weights32, precision=lax.Precision.HIGHEST)
        running = running.at[:, row_list].add(contrib)
        grads = jnp.einsum('tki,tj->kij', picked_rows, slopes32, precision=lax.Precision.HIGHEST)
        return (running, (activated, grads))
    start_grad = jnp.zeros((num_tokens, RB, BLK), jnp.float32)
    total_grad, (activated, block_grad) = lax.scan(column, start_grad, (block_values, block_rows, cot_columns))
    gelu_out = jnp.transpose(activated, (1, 0, 2)).reshape(num_tokens, FF)
    input_grad = total_grad.reshape(num_tokens, D).astype(jnp.bfloat16)
    return (gelu_out, input_grad, block_grad)
```

```python
import functools

import jax
import jax.numpy as jnp
from jax import lax
from jax.experimental import pallas as pl
from jax.experimental.pallas import tpu as pltpu
from jax.sharding import PartitionSpec as P

NX, NY, NZ, NC, NM = 4, 2, 12, 2, 4
BLK, KB, RB, CB = 128, 20, 72, 2
SH = 48
ZB = 4
NB = NZ // ZB
OWN = KB // NM
FAR_FIRST = (2, 1, 3)
Z_ORDER = (1, 11, 2, 10, 3, 9, 4, 8, 5, 7, 6)
F32, BF16 = jnp.float32, jnp.bfloat16
C0 = 0.7978845608028654
C1 = 0.044715


def coords():
    d = lax.axis_index("dp")
    c = lax.rem(d, NC)
    z = lax.rem(lax.div(d, NC), NZ)
    y = lax.rem(lax.div(d, NC * NZ), NY)
    x = lax.div(d, NC * NZ * NY)
    return x, y, z, c, lax.axis_index("mp")


def device(x, y, z, c, m):
    return (((x * NY + y) * NZ + z) * NC + c, m)


def remote(src, dst, send, recv, to):
    return pltpu.make_async_remote_copy(
        src_ref=src, dst_ref=dst, send_sem=send, recv_sem=recv,
        device_id=to, device_id_type=pl.DeviceIdType.MESH,
    )


def kernel(
    rows_ref, inv_ref, xt_ref, cot_ref, w_hbm,
    gelu_ref, dx_ref, bg_ref,
    X, W, XF, XP, SL, D, S, XS, XR, OX, YS, YR, OY, ZS, ZR,
    GS1, GR1, GS2, GR2, GP,
    wsem, zs, zr, ys, yr, xs, xr, bs, br,
    ss, sr, rxs, rxr, rys, ryr, rzs, rzr, g1s, g1r, g2s, g2r,
):
    x, y, z, c, m = coords()
    oy, oc = 1 - y, 1 - c
    xa = [x] + [lax.rem(x + j, NX) for j in range(1, NX)]
    za = [z] + [lax.rem(z + k, NZ) for k in range(1, NZ)]
    m1, m2, m3 = (lax.rem(m + k, NM) for k in (1, 2, 3))
    to_x = [None] + [device(xa[j], y, z, c, m) for j in range(1, NX)]
    to_z = [None] + [device(x, y, za[k], c, m) for k in range(1, NZ)]
    to_y = device(x, oy, z, c, m)
    to_c = device(x, y, z, oc, m)
    to_up, to_down = device(x, y, z, c, m1), device(x, y, z, c, m3)

    wcopy = pltpu.make_async_copy(w_hbm, W.at[:, pl.ds(0, KB)], wsem)
    wcopy.start()

    barrier = pltpu.get_barrier_semaphore()
    partners = to_z[1:] + to_x[1:] + [to_y, to_c, to_up, to_down]
    for d in partners:
        pl.semaphore_signal(barrier, inc=1, device_id=d, device_id_type=pl.DeviceIdType.MESH)
    pl.semaphore_wait(barrier, len(partners))

    started = []

    def go(copy):
        copy.start()
        started.append(copy)

    for k in Z_ORDER:
        go(remote(xt_ref, X.at[x, y, z, c], zs.at[k - 1], zr.at[z], to_z[k]))
    X[x, y, z, c] = xt_ref[...]
    b0 = lax.div(z, ZB)
    blocks = [lax.rem(b0 + i, NB) for i in range(NB)]

    def part(xx, yy, i, cc):
        return X.at[xx, yy, pl.ds(blocks[i] * ZB, ZB), cc]

    def spread(yy, p, i):
        piece = part(x, yy, i, c)
        for j in FAR_FIRST:
            go(remote(piece, piece, xs.at[j - 1, p, i], xr.at[j - 1, p, i], to_x[j]))
        go(remote(piece, piece, bs.at[0, p, i], br.at[0, p, i], to_c))

    def from_y(i):
        piece = part(x, oy, i, c)
        remote(piece, piece, ys.at[i], yr.at[i], to_y).wait_recv()
        spread(oy, 1, i)

    for i in range(NB):
        for n in range(ZB):
            zz = blocks[i] * ZB + n

            @pl.when(zz != z)
            def _():
                piece = X.at[x, y, zz, c]
                remote(piece, piece, zs.at[0], zr.at[zz], to_y).wait_recv()

        piece = part(x, y, i, c)
        go(remote(piece, piece, ys.at[i], yr.at[i], to_y))
        spread(y, 0, i)
        if i:
            from_y(i - 1)
    from_y(NB - 1)
    wcopy.wait()
    for cb in range(CB):
        W[cb, KB] = jnp.zeros((BLK, BLK), BF16)
    for p in range(NY):
        for i in range(NB):
            for j in (1, 3, 2):
                piece = part(xa[NX - j], (y, oy)[p], i, c)
                remote(piece, piece, xs.at[j - 1, p, i], xr.at[j - 1, p, i], to_y).wait_recv()
                go(remote(piece, piece, bs.at[j, p, i], br.at[j, p, i], to_c))
    for p in range(NY):
        for i in range(NB):
            for j in (0, 1, 3, 2):
                piece = part(xa[(NX - j) % NX], (y, oy)[p], i, oc)
                remote(piece, piece, bs.at[j, p, i], br.at[j, p, i], to_c).wait_recv()

    XF[...] = X[...].reshape(RB, BLK, BLK)
    for cb in range(CB):
        for k in range(KB):
            XP[cb, pl.ds(k * BLK, BLK)] = XF[rows_ref[cb, k]]
    for cb in range(CB):
        cols = pl.ds(cb * BLK, BLK)
        v = lax.dot_general(
            XP[cb], W[cb, :KB].reshape(KB * BLK, BLK), (((0,), (0,)), ((), ())),
            preferred_element_type=F32,
        )
        t = jnp.tanh(C0 * (v + C1 * (v * v * v)))
        gelu_ref[:, cols] = (0.5 * v * (1.0 + t)).astype(BF16)
        slope = 0.5 * (1.0 + t) + 0.5 * v * (1.0 - t * t) * (C0 * (1.0 + 3.0 * C1 * (v * v)))
        SL[:, cols] = (cot_ref[:, cols].astype(F32) * slope).astype(BF16)

    def grads(cb, group):
        return jnp.dot(
            XP[cb, pl.ds(group * (OWN * BLK), OWN * BLK)], SL[:, cb * BLK : (cb + 1) * BLK],
            preferred_element_type=F32,
        )

    GS1[0] = grads(0, m2).astype(BF16)
    go(remote(GS1.at[0], GR1.at[0], g1s.at[0], g1r.at[0], to_up))
    GS1[1] = grads(1, m2).astype(BF16)
    go(remote(GS1.at[1], GR1.at[1], g1s.at[1], g1r.at[1], to_down))
    GS2[0, 1] = grads(1, m1).astype(BF16)
    go(remote(GS2.at[0, 1], GR2.at[0, 1], g2s.at[0, 1], g2r.at[0, 1], to_up))
    GS2[1, 0] = grads(0, m3).astype(BF16)
    go(remote(GS2.at[1, 0], GR2.at[1, 0], g2s.at[1, 0], g2r.at[1, 0], to_down))
    GP[0] = grads(0, m1)
    GP[1] = grads(1, m3)

    def terms(j):
        xx = xa[j]

        def step(g, carry):
            made = []
            for n in range(3):
                r = xx * (RB // NX) + g * 3 + n
                pair = jnp.concatenate([W[0, inv_ref[0, r]], W[1, inv_ref[1, r]]], axis=1)
                made.append(
                    lax.dot_general(pair, SL[...], (((1,), (1,)), ((), ())), preferred_element_type=F32)
                )
            both = jnp.concatenate(made, axis=0).reshape(ZB, NC, SH, BLK).astype(BF16)
            D[xx, lax.div(g, NB), pl.ds(lax.rem(g, NB) * ZB, ZB)] = both
            return carry

        lax.fori_loop(0, NY * NB, step, 0)
        go(remote(D.at[xx, :, :, oc], S.at[j], ss.at[j], sr.at[j], to_c))

    def paired(j):
        remote(D.at[xa[j], :, :, oc], S.at[j], ss.at[j], sr.at[j], to_c).wait_recv()

    def both_cores(j, p):
        yy = (y, oy)[p]
        return D[xa[j], yy, :, c].astype(F32) + S[j, yy].astype(F32)

    def along_x(j):
        paired(j)
        for p in (1, 0):
            XS[j - 1, p] = both_cores(j, p).astype(BF16)
            go(remote(XS.at[j - 1, p], XR.at[j - 1, p], rxs.at[j - 1, p], rxr.at[j - 1, p], to_x[j]))

    terms(2)
    terms(1)
    along_x(2)
    terms(3)
    along_x(1)
    terms(0)
    along_x(3)
    paired(0)
    for p in range(NY):
        OX[p] = both_cores(0, p)
    for cb in range(CB):
        bg_ref[cb] = grads(cb, m).reshape(OWN, BLK, BLK)

    def from_x(p):
        total = OX[p]
        for j in range(1, NX):
            remote(XS.at[j - 1, p], XR.at[j - 1, p], rxs.at[j - 1, p], rxr.at[j - 1, p], to_y).wait_recv()
            total = total + XR[j - 1, p].astype(F32)
        return total

    def second(side, cb, to):
        remote(GS1.at[cb], GR1.at[cb], g1s.at[cb], g1r.at[cb], to).wait_recv()
        GS2[side, cb] = (GP[cb] + GR1[cb].astype(F32)).astype(BF16)
        go(remote(GS2.at[side, cb], GR2.at[side, cb], g2s.at[side, cb], g2r.at[side, cb], to))

    second(0, 0, to_up)
    second(1, 1, to_down)
    YS[...] = from_x(1).astype(BF16)
    go(remote(YS, YR, rys, ryr, to_y))
    OY[...] = from_x(0)
    remote(YS, YR, rys, ryr, to_y).wait_recv()
    OY[...] = OY[...] + YR[...].astype(F32)
    ZS[...] = OY[...].astype(BF16)
    for k in Z_ORDER:
        go(remote(ZS.at[za[k]], ZR.at[k - 1], rzs.at[k - 1], rzr.at[k - 1], to_z[k]))
    dx = OY[z]
    for k in Z_ORDER:
        remote(ZS.at[za[k]], ZR.at[k - 1], rzs.at[k - 1], rzr.at[k - 1], to_y).wait_recv()
        dx = dx + ZR[k - 1].astype(F32)
    dx_ref[...] = dx.astype(BF16)

    for cb in range(CB):
        total = bg_ref[cb]
        for side in range(2):
            remote(GS2.at[side, cb], GR2.at[side, cb], g2s.at[side, cb], g2r.at[side, cb], to_up).wait_recv()
            total = total + GR2[side, cb].astype(F32).reshape(OWN, BLK, BLK)
        bg_ref[cb] = total
    for copy in started:
        copy.wait_send()


def body(activations, block_values, block_rows, cotangent):
    tokens = activations.shape[0]
    slots = jnp.arange(KB, dtype=jnp.int32) - KB
    named = block_rows[:, None, :] == jnp.arange(RB, dtype=jnp.int32)[None, :, None]
    inverse = KB + jnp.sum(jnp.where(named, slots, 0), axis=2, dtype=jnp.int32)
    smem, vmem = pl.BlockSpec(memory_space=pltpu.SMEM), pl.BlockSpec(memory_space=pltpu.VMEM)
    dma = pltpu.SemaphoreType.DMA
    column = (OWN * BLK, BLK)
    gelu_out, dx, block_grad = pl.pallas_call(
        kernel,
        name="sparse_up_both_ways",
        out_shape=(
            jax.ShapeDtypeStruct((tokens, CB * BLK), BF16),
            jax.ShapeDtypeStruct((SH, tokens), BF16),
            jax.ShapeDtypeStruct((CB, OWN, BLK, BLK), F32),
        ),
        in_specs=[smem, smem, vmem, vmem, pl.BlockSpec(memory_space=pl.ANY)],
        out_specs=(vmem, vmem, vmem),
        scratch_shapes=[
            pltpu.VMEM((NX, NY, NZ, NC, SH, BLK), BF16),
            pltpu.VMEM((CB, KB + 1, BLK, BLK), BF16),
            pltpu.VMEM((RB, BLK, BLK), BF16),
            pltpu.VMEM((CB, KB * BLK, BLK), BF16),
            pltpu.VMEM((BLK, CB * BLK), BF16),
            pltpu.VMEM((NX, NY, NZ, NC, SH, BLK), BF16),
            pltpu.VMEM((NX, NY, NZ, SH, BLK), BF16),
            pltpu.VMEM((NX - 1, NY, NZ, SH, BLK), BF16),
            pltpu.VMEM((NX - 1, NY, NZ, SH, BLK), BF16),
            pltpu.VMEM((NY, NZ, SH, BLK), F32),
            pltpu.VMEM((NZ, SH, BLK), BF16),
            pltpu.VMEM((NZ, SH, BLK), BF16),
            pltpu.VMEM((NZ, SH, BLK), F32),
            pltpu.VMEM((NZ, SH, BLK), BF16),
            pltpu.VMEM((NZ - 1, SH, BLK), BF16),
            pltpu.VMEM((2, *column), BF16),
            pltpu.VMEM((2, *column), BF16),
            pltpu.VMEM((2, CB, *column), BF16),
            pltpu.VMEM((2, CB, *column), BF16),
            pltpu.VMEM((2, *column), F32),
            dma,
            dma((NZ - 1,)), dma((NZ,)),
            dma((NB,)), dma((NB,)),
            dma((NX - 1, NY, NB)), dma((NX - 1, NY, NB)),
            dma((NX, NY, NB)), dma((NX, NY, NB)),
            dma((NX,)), dma((NX,)),
            dma((NX - 1, NY)), dma((NX - 1, NY)),
            dma, dma,
            dma((NZ - 1,)), dma((NZ - 1,)),
            dma((2,)), dma((2,)),
            dma((2, CB)), dma((2, CB)),
        ],
        compiler_params=pltpu.CompilerParams(
            collective_id=0, has_side_effects=True, vmem_limit_bytes=48 << 20
        ),
    )(block_rows, inverse, activations.T, cotangent, block_values)
    return gelu_out, dx.T, block_grad


def solution(mesh):
    in_specs = (P("mp", "dp"), P("dp", None, None, None), P("dp", None), P("mp", "dp"))
    out_specs = (P("mp", "dp"), P("mp", "dp"), P("dp", "mp", None, None))
    return jax.shard_map(body, mesh=mesh, in_specs=in_specs, out_specs=out_specs, check_vma=False)
```

```python
import functools

import jax
import jax.numpy as jnp
from jax import lax
from jax.experimental import pallas as pl
from jax.experimental.pallas import tpu as pltpu
from jax.sharding import PartitionSpec as P

NX, NY, NZ, NC, NM = 4, 2, 12, 2, 4
BLK, KB, RB, CB = 128, 20, 72, 2
SH = 48
ZB = 4
RANK = (0, 1, 11, 2, 10, 3, 9, 4, 8, 5, 7, 6)
GROUPS = ((0, 1), (1, 2), (3, 4), (7, 5))
NG = len(GROUPS)
X_FIRST = (2,)
OWN = KB // NM
FAR_FIRST = (2, 1, 3)
F32, BF16 = jnp.float32, jnp.bfloat16
C0 = 0.7978845608028654
C1 = 0.044715


def coords():
    d = lax.axis_index("dp")
    c = lax.rem(d, NC)
    z = lax.rem(lax.div(d, NC), NZ)
    y = lax.rem(lax.div(d, NC * NZ), NY)
    x = lax.div(d, NC * NZ * NY)
    return x, y, z, c, lax.axis_index("mp")


def device(x, y, z, c, m):
    return (((x * NY + y) * NZ + z) * NC + c, m)


def remote(src, dst, send, recv, to):
    return pltpu.make_async_remote_copy(
        src_ref=src, dst_ref=dst, send_sem=send, recv_sem=recv,
        device_id=to, device_id_type=pl.DeviceIdType.MESH,
    )


def kernel(
    rows_hbm, xt_hbm, cot_hbm, w_hbm,
    gelu_ref, dx_ref, bg_ref,
    X, W, COT, XQ, XF, XP, SL, D, S, XS, XR, OX, YS, YR, ZR0, ZS, ZR,
    GS1, GR1, GS2, GR2, GP, IV, ROWS, INV,
    isem, zs, zr, ys, yr, xs, xr, bs, br,
    ss, sr, rxs, rxr, rys, ryr, rzs, rzr, g1s, g1r, g2s, g2r,
):
    x, y, z, c, m = coords()
    oy, oc = 1 - y, 1 - c
    side = (y, oy)
    xa = [x] + [lax.rem(x + j, NX) for j in range(1, NX)]
    za = [z] + [lax.rem(z + k, NZ) for k in range(1, NZ)]
    m1, m2, m3 = (lax.rem(m + k, NM) for k in (1, 2, 3))
    to_x = [None] + [device(xa[j], y, z, c, m) for j in range(1, NX)]
    to_z = [None] + [device(x, y, za[k], c, m) for k in range(1, NZ)]
    to_y = device(x, oy, z, c, m)
    to_c = device(x, y, z, oc, m)
    to_up, to_down = device(x, y, z, c, m1), device(x, y, z, c, m3)

    own_x = pltpu.make_async_copy(xt_hbm, X.at[0, 0, 0, 0], isem.at[0])
    rows_in = pltpu.make_async_copy(rows_hbm, ROWS, isem.at[1])
    w_in = pltpu.make_async_copy(w_hbm, W.at[:, pl.ds(0, KB)], isem.at[2])
    cot_in = pltpu.make_async_copy(cot_hbm, COT, isem.at[3])
    for copy in (own_x, rows_in, w_in, cot_in):
        copy.start()

    barrier = pltpu.get_barrier_semaphore()
    partners = to_z[1:] + to_x[1:] + [to_y, to_c, to_up, to_down]
    for d in partners:
        pl.semaphore_signal(barrier, inc=1, device_id=d, device_id_type=pl.DeviceIdType.MESH)
    own_x.wait()
    pl.semaphore_wait(barrier, len(partners))

    started = []

    def go(copy):
        copy.start()
        started.append(copy)

    def drain():
        for copy in started:
            copy.wait_send()
        started.clear()

    def ranks(i):
        return range(GROUPS[i][0], sum(GROUPS[i]))

    def part(j, p, i, cc=0):
        return X.at[j, p, pl.ds(*GROUPS[i]), cc]

    def z_in(n, to):
        back = RANK.index((NZ - RANK[n]) % NZ)
        return remote(X.at[0, 0, 0, 0], X.at[0, 0, back, 0], zs.at[back], zr.at[back], to)

    def x_in(j, p, i):
        return remote(part(0, p, i), part(j, p, i), xs.at[j - 1, p, i], xr.at[j - 1, p, i], to_x[j])

    def y_in(j, i):
        return remote(part(j, 0, i), part(j, 1, i), ys.at[j, i], yr.at[j, i], to_y)

    def c_in(j, p, i):
        return remote(part(j, p, i), part(j, p, i, 1), bs.at[j, p, i], br.at[j, p, i], to_c)

    def send_x(p, i):
        for j in FAR_FIRST:
            go(x_in(j, p, i))

    def y_then_x(i):
        y_in(0, i).wait_recv()
        send_x(1, i)
        go(c_in(0, 1, i))

    def x_then_y(i):
        for j in (1, 3, 2):
            x_in(j, 0, i).wait_recv()
            go(y_in(j, i))
            go(c_in(j, 0, i))

    for n in range(1, NZ):
        go(z_in(n, to_z[RANK[n]]))
    waiting = []
    for i in range(NG):
        for n in ranks(i):
            if n:
                z_in(RANK.index((NZ - RANK[n]) % NZ), to_y).wait_recv()
        go(y_in(0, i))
        send_x(0, i)
        go(c_in(0, 0, i))
        if waiting:
            waiting.pop(0)()
        waiting.append(functools.partial(x_then_y if i in X_FIRST else y_then_x, i))
    for step in waiting:
        step()

    rows_in.wait()
    lanes = lax.broadcasted_iota(jnp.int32, (1, BLK), 1)
    for cb in range(CB):
        found = jnp.full((1, BLK), KB, jnp.int32)
        for k in range(KB):
            found = jnp.where(lanes == ROWS[cb, k], k, found)
        IV[pl.ds(cb, 1)] = found
    inv_in = pltpu.make_async_copy(IV, INV, isem.at[1])
    inv_in.start()
    w_in.wait()
    cot_in.wait()
    for cb in range(CB):
        W[cb, KB] = jnp.zeros((BLK, BLK), BF16)
    inv_in.wait()

    for i in range(NG):
        for j in (1, 3, 2):
            for p in range(NY):
                if i not in X_FIRST:
                    x_in(j, p, i).wait_recv()
                    go(c_in(j, p, i))
    for i in X_FIRST:
        for j in (0, 1, 3, 2):
            y_in(j, i).wait_recv()
            go(c_in(j, 1, i))
    for i in range(NG):
        for j in (0, 1, 3, 2):
            for p in range(NY):
                c_in(j, p, i).wait_recv()

    for j in range(NX):
        for p in range(NY):
            for n in range(NZ):
                XQ[xa[(NX - j) % NX], side[p], za[RANK[n]], c] = X[j, p, n, 0]
                XQ[xa[(NX - j) % NX], side[p], za[RANK[n]], oc] = X[j, p, n, 1]
    XF[...] = XQ[...].reshape(RB, BLK, BLK)
    for cb in range(CB):
        for k in range(KB):
            XP[cb, pl.ds(k * BLK, BLK)] = XF[ROWS[cb, k]]
    for cb in range(CB):
        cols = pl.ds(cb * BLK, BLK)
        v = lax.dot_general(
            XP[cb], W[cb, :KB].reshape(KB * BLK, BLK), (((0,), (0,)), ((), ())),
            preferred_element_type=F32,
        )
        t = jnp.tanh(C0 * (v + C1 * (v * v * v)))
        gelu_ref[:, cols] = (0.5 * v * (1.0 + t)).astype(BF16)
        slope = 0.5 * (1.0 + t) + 0.5 * v * (1.0 - t * t) * (C0 * (1.0 + 3.0 * C1 * (v * v)))
        SL[:, cols] = (COT[:, cols].astype(F32) * slope).astype(BF16)

    def grads(cb, group):
        return jnp.dot(
            XP[cb, pl.ds(group * (OWN * BLK), OWN * BLK)], SL[:, cb * BLK : (cb + 1) * BLK],
            preferred_element_type=F32,
        )

    def g1(cb, to):
        return remote(GS1.at[cb], GR1.at[cb], g1s.at[cb], g1r.at[cb], to)

    def g2(way, cb, to):
        return remote(GS2.at[way, cb], GR2.at[way, cb], g2s.at[way, cb], g2r.at[way, cb], to)

    GS1[0] = grads(0, m2).astype(BF16)
    go(g1(0, to_up))
    GS1[1] = grads(1, m2).astype(BF16)
    go(g1(1, to_down))

    def pair_copy(j, p):
        return remote(D.at[xa[j], side[p], :, oc], S.at[j, p], ss.at[j, p], sr.at[j, p], to_c)

    def terms(j, p):
        first = xa[j] * (RB // NX) + side[p] * (RB // NX // NY)

        def step(g, carry):
            made = []
            for n in range(3):
                r = first + g * 3 + n
                pair = jnp.concatenate([W[0, INV[0, r]], W[1, INV[1, r]]], axis=1)
                made.append(
                    lax.dot_general(pair, SL[...], (((1,), (1,)), ((), ())), preferred_element_type=F32)
                )
            both = jnp.concatenate(made, axis=0).reshape(ZB, NC, SH, BLK).astype(BF16)
            D[xa[j], side[p], pl.ds(g * ZB, ZB)] = both
            return carry

        lax.fori_loop(0, NZ // ZB, step, 0)
        go(pair_copy(j, p))

    def both_cores(j, p, n):
        zz = za[RANK[n]]
        return D[xa[j], side[p], zz, c].astype(F32) + S[j, p, zz].astype(F32)

    def x_copy(j, p, i):
        at = pl.ds(*GROUPS[i])
        return remote(
            XS.at[j - 1, p, at], XR.at[j - 1, p, at], rxs.at[j - 1, p, i], rxr.at[j - 1, p, i], to_x[j]
        )

    def y_copy(i):
        at = pl.ds(*GROUPS[i])
        return remote(YS.at[at], YR.at[at], rys.at[i], ryr.at[i], to_y)

    def z_copy(n, to):
        back = RANK.index((NZ - RANK[n]) % NZ)
        return remote(ZS.at[n], ZR.at[back], rzs.at[n], rzr.at[back], to)

    def second(way, cb, to):
        g1(cb, to).wait_recv()
        GS2[way, cb] = (GP[cb] + GR1[cb].astype(F32)).astype(BF16)
        go(g2(way, cb, to))

    far_groups = range(NG - 1, -1, -1)

    def along_x(p, i):
        for j in FAR_FIRST:
            for n in ranks(i):
                XS[j - 1, p, n] = both_cores(j, p, n).astype(BF16)
            go(x_copy(j, p, i))

    for p in (1, 0):
        for j in (2, 1, 3, 0):
            terms(j, p)
    for p in (1, 0):
        for j in FAR_FIRST:
            pair_copy(j, p).wait_recv()
        for i in far_groups:
            if p == 1:
                along_x(1, i)
    for i in far_groups:
        along_x(0, i)
    GS2[0, 1] = grads(1, m1).astype(BF16)
    go(g2(0, 1, to_up))
    GS2[1, 0] = grads(0, m3).astype(BF16)
    go(g2(1, 0, to_down))
    for p in (1, 0):
        pair_copy(0, p).wait_recv()
        for n in range(NZ):
            OX[p, n] = both_cores(0, p, n)
    GP[0] = grads(0, m1)
    GP[1] = grads(1, m3)
    for cb in range(CB):
        bg_ref[cb] = grads(cb, m).reshape(OWN, BLK, BLK)

    def from_x(p, i):
        at = pl.ds(*GROUPS[i])
        total = OX[p, at]
        for j in FAR_FIRST:
            x_copy(j, p, i).wait_recv()
            total = total + XR[j - 1, p, at].astype(F32)
        return total

    for i in far_groups:
        YS[pl.ds(*GROUPS[i])] = from_x(1, i).astype(BF16)
        go(y_copy(i))
    for i in far_groups:
        at = pl.ds(*GROUPS[i])
        total = from_x(0, i)
        y_copy(i).wait_recv()
        total = total + YR[at].astype(F32)
        if i == 0:
            ZR0[...] = total
            continue
        ZS[at] = total.astype(BF16)
        for n in ranks(i):
            go(z_copy(n, to_z[RANK[n]]))
        if i == NG - 1:
            second(0, 0, to_up)
            second(1, 1, to_down)
    dx = ZR0[0]

    def add(way, cb):
        g2(way, cb, to_up).wait_recv()
        bg_ref[cb] = bg_ref[cb] + GR2[way, cb].astype(F32).reshape(OWN, BLK, BLK)

    for n in range(1, NZ):
        z_copy(RANK.index((NZ - RANK[n]) % NZ), to_y).wait_recv()
        dx = dx + ZR[n].astype(F32)
    dx_ref[...] = dx.astype(BF16)
    add(0, 1)
    add(1, 0)
    add(0, 0)
    add(1, 1)
    drain()


def body(activations, block_values, block_rows, cotangent):
    tokens = activations.shape[0]
    hbm, vmem = pl.BlockSpec(memory_space=pltpu.HBM), pl.BlockSpec(memory_space=pltpu.VMEM)
    dma = pltpu.SemaphoreType.DMA
    column = (OWN * BLK, BLK)
    gelu_out, dx, block_grad = pl.pallas_call(
        kernel,
        name="sparse_up_both_ways",
        out_shape=(
            jax.ShapeDtypeStruct((tokens, CB * BLK), BF16),
            jax.ShapeDtypeStruct((SH, tokens), BF16),
            jax.ShapeDtypeStruct((CB, OWN, BLK, BLK), F32),
        ),
        in_specs=[hbm] * 4,
        out_specs=(vmem, vmem, vmem),
        scratch_shapes=[
            pltpu.VMEM((NX, NY, NZ, NC, SH, BLK), BF16),
            pltpu.VMEM((CB, KB + 1, BLK, BLK), BF16),
            pltpu.VMEM((BLK, CB * BLK), BF16),
            pltpu.VMEM((NX, NY, NZ, NC, SH, BLK), BF16),
            pltpu.VMEM((RB, BLK, BLK), BF16),
            pltpu.VMEM((CB, KB * BLK, BLK), BF16),
            pltpu.VMEM((BLK, CB * BLK), BF16),
            pltpu.VMEM((NX, NY, NZ, NC, SH, BLK), BF16),
            pltpu.VMEM((NX, NY, NZ, SH, BLK), BF16),
            pltpu.VMEM((NX - 1, NY, NZ, SH, BLK), BF16),
            pltpu.VMEM((NX - 1, NY, NZ, SH, BLK), BF16),
            pltpu.VMEM((NY, NZ, SH, BLK), F32),
            pltpu.VMEM((NZ, SH, BLK), BF16),
            pltpu.VMEM((NZ, SH, BLK), BF16),
            pltpu.VMEM((1, SH, BLK), F32),
            pltpu.VMEM((NZ, SH, BLK), BF16),
            pltpu.VMEM((NZ, SH, BLK), BF16),
            pltpu.VMEM((2, *column), BF16),
            pltpu.VMEM((2, *column), BF16),
            pltpu.VMEM((2, CB, *column), BF16),
            pltpu.VMEM((2, CB, *column), BF16),
            pltpu.VMEM((2, *column), F32),
            pltpu.VMEM((CB, BLK), jnp.int32),
            pltpu.SMEM((CB, KB), jnp.int32),
            pltpu.SMEM((CB, BLK), jnp.int32),
            dma((4,)),
            dma((NZ,)), dma((NZ,)),
            dma((NX, NG)), dma((NX, NG)),
            dma((NX - 1, NY, NG)), dma((NX - 1, NY, NG)),
            dma((NX, NY, NG)), dma((NX, NY, NG)),
            dma((NX, NY)), dma((NX, NY)),
            dma((NX - 1, NY, NG)), dma((NX - 1, NY, NG)),
            dma((NG,)), dma((NG,)),
            dma((NZ,)), dma((NZ,)),
            dma((2,)), dma((2,)),
            dma((2, CB)), dma((2, CB)),
        ],
        compiler_params=pltpu.CompilerParams(
            collective_id=0, has_side_effects=True, vmem_limit_bytes=48 << 20
        ),
    )(block_rows, activations.T, cotangent, block_values)
    return gelu_out, dx.T, block_grad


def solution(mesh):
    in_specs = (P("mp", "dp"), P("dp", None, None, None), P("dp", None), P("mp", "dp"))
    out_specs = (P("mp", "dp"), P("mp", "dp"), P("dp", "mp", None, None))
    return jax.shard_map(body, mesh=mesh, in_specs=in_specs, out_specs=out_specs, check_vma=False)
```

```python
import functools

import jax
import jax.numpy as jnp
from jax import lax
from jax.experimental import pallas as pl
from jax.experimental.pallas import tpu as pltpu
from jax.sharding import PartitionSpec as P

NX, NY, NZ, NC, NM = 4, 2, 12, 2, 4
BLK, KB, RB, CB = 128, 20, 72, 2
SH = 48
ZB = 4
RANK = (0, 1, 11, 2, 10, 3, 9, 4, 8, 5, 7, 6)
GROUPS = ((0, 1), (1, 2), (3, 4), (7, 5))
NG = len(GROUPS)
OWN = KB // NM
FAR_FIRST = (2, 1, 3)
F32, BF16 = jnp.float32, jnp.bfloat16
C0 = 0.7978845608028654
C1 = 0.044715


def coords():
    d = lax.axis_index("dp")
    c = lax.rem(d, NC)
    z = lax.rem(lax.div(d, NC), NZ)
    y = lax.rem(lax.div(d, NC * NZ), NY)
    x = lax.div(d, NC * NZ * NY)
    return x, y, z, c, lax.axis_index("mp")


def device(x, y, z, c, m):
    return (((x * NY + y) * NZ + z) * NC + c, m)


def remote(src, dst, send, recv, to):
    return pltpu.make_async_remote_copy(
        src_ref=src, dst_ref=dst, send_sem=send, recv_sem=recv,
        device_id=to, device_id_type=pl.DeviceIdType.MESH,
    )


def kernel(
    rows_hbm, xt_hbm, cot_hbm, w_hbm,
    gelu_ref, dx_ref, bg_ref,
    X, W, COT, XQ, XF, XP, SL, SLT, D, S, XS, XR, OX, YS, YR, ZR0, ZS, ZR,
    GS1, GR1, GS2, GR2, GP, IV, ROWS, INV,
    isem, zs, zr, ys, yr, xs, xr, bs, br,
    ss, sr, rxs, rxr, rys, ryr, rzs, rzr, g1s, g1r, g2s, g2r,
):
    x, y, z, c, m = coords()
    oy, oc = 1 - y, 1 - c
    side = (y, oy)
    xa = [x] + [lax.rem(x + j, NX) for j in range(1, NX)]
    za = [z] + [lax.rem(z + k, NZ) for k in range(1, NZ)]
    m1, m2, m3 = (lax.rem(m + k, NM) for k in (1, 2, 3))
    to_x = [None] + [device(xa[j], y, z, c, m) for j in range(1, NX)]
    to_z = [None] + [device(x, y, za[k], c, m) for k in range(1, NZ)]
    to_y = device(x, oy, z, c, m)
    to_c = device(x, y, z, oc, m)
    to_up, to_down = device(x, y, z, c, m1), device(x, y, z, c, m3)

    own_x = pltpu.make_async_copy(xt_hbm, X.at[0, 0, 0, 0], isem.at[0])
    rows_in = pltpu.make_async_copy(rows_hbm, ROWS, isem.at[1])
    w_in = pltpu.make_async_copy(w_hbm, W.at[:, pl.ds(0, KB)], isem.at[2])
    cot_in = pltpu.make_async_copy(cot_hbm, COT, isem.at[3])
    for copy in (own_x, rows_in, w_in, cot_in):
        copy.start()

    barrier = pltpu.get_barrier_semaphore()
    partners = to_z[1:] + to_x[1:] + [to_y, to_c, to_up, to_down]
    for d in partners:
        pl.semaphore_signal(barrier, inc=1, device_id=d, device_id_type=pl.DeviceIdType.MESH)
    own_x.wait()
    pl.semaphore_wait(barrier, len(partners))

    started = []

    def go(copy):
        copy.start()
        started.append(copy)

    def drain():
        for copy in started:
            copy.wait_send()
        started.clear()

    def ranks(i):
        return range(GROUPS[i][0], sum(GROUPS[i]))

    def part(j, p, i, cc=0):
        return X.at[j, p, pl.ds(*GROUPS[i]), cc]

    def z_in(n, to):
        back = RANK.index((NZ - RANK[n]) % NZ)
        return remote(X.at[0, 0, 0, 0], X.at[0, 0, back, 0], zs.at[back], zr.at[back], to)

    def x_in(j, p, i):
        return remote(part(0, p, i), part(j, p, i), xs.at[j - 1, p, i], xr.at[j - 1, p, i], to_x[j])

    def y_in(j, i):
        return remote(part(j, 0, i), part(j, 1, i), ys.at[j, i], yr.at[j, i], to_y)

    def c_in(j, p, i):
        return remote(part(j, p, i), part(j, p, i, 1), bs.at[j, p, i], br.at[j, p, i], to_c)

    def send_x(p, i):
        for j in FAR_FIRST:
            go(x_in(j, p, i))

    def y_then_x(i):
        y_in(0, i).wait_recv()
        send_x(1, i)
        go(c_in(0, 1, i))

    def x_then_y(i):
        for j in (1, 3, 2):
            x_in(j, 0, i).wait_recv()
            go(y_in(j, i))
            go(c_in(j, 0, i))

    for n in range(1, NZ):
        go(z_in(n, to_z[RANK[n]]))
    def along_z(i):
        for n in ranks(i):
            if n:
                z_in(RANK.index((NZ - RANK[n]) % NZ), to_y).wait_recv()
        go(y_in(0, i))
        send_x(0, i)
        go(c_in(0, 0, i))

    def x_to_core(p, i):
        for j in (1, 3, 2):
            x_in(j, p, i).wait_recv()
            go(c_in(j, p, i))

    along_z(0)
    along_z(1)
    y_then_x(0)
    along_z(2)
    y_then_x(1)
    x_to_core(0, 0)
    x_to_core(1, 0)
    x_to_core(0, 1)
    along_z(3)
    x_then_y(2)
    y_then_x(3)
    x_to_core(1, 1)

    rows_in.wait()
    lanes = lax.broadcasted_iota(jnp.int32, (1, BLK), 1)
    for cb in range(CB):
        found = jnp.full((1, BLK), KB, jnp.int32)
        for k in range(KB):
            found = jnp.where(lanes == ROWS[cb, k], k, found)
        IV[pl.ds(cb, 1)] = found
    inv_in = pltpu.make_async_copy(IV, INV, isem.at[1])
    inv_in.start()
    w_in.wait()
    cot_in.wait()
    for cb in range(CB):
        W[cb, KB] = jnp.zeros((BLK, BLK), BF16)
    inv_in.wait()

    for j in (0, 1, 3, 2):
        y_in(j, 2).wait_recv()
        go(c_in(j, 1, 2))
    x_to_core(0, 3)
    x_to_core(1, 3)
    for i in range(NG):
        for j in (0, 1, 3, 2):
            for p in range(NY):
                c_in(j, p, i).wait_recv()

    for j in range(NX):
        for p in range(NY):
            for n in range(NZ):
                XQ[xa[(NX - j) % NX], side[p], za[RANK[n]], c] = X[j, p, n, 0]
                XQ[xa[(NX - j) % NX], side[p], za[RANK[n]], oc] = X[j, p, n, 1]
    XF[...] = XQ[...].reshape(RB, BLK, BLK)
    for cb in range(CB):
        for k in range(KB):
            XP[cb, pl.ds(k * BLK, BLK)] = XF[ROWS[cb, k]]
    for cb in range(CB):
        cols = pl.ds(cb * BLK, BLK)
        v = lax.dot_general(
            XP[cb], W[cb, :KB].reshape(KB * BLK, BLK), (((0,), (0,)), ((), ())),
            preferred_element_type=F32,
        )
        t = jnp.tanh(C0 * (v + C1 * (v * v * v)))
        gelu_ref[:, cols] = (0.5 * v * (1.0 + t)).astype(BF16)
        slope = 0.5 * (1.0 + t) + 0.5 * v * (1.0 - t * t) * (C0 * (1.0 + 3.0 * C1 * (v * v)))
        SL[:, cols] = (COT[:, cols].astype(F32) * slope).astype(BF16)

    def grads(cb, group):
        return jnp.dot(
            XP[cb, pl.ds(group * (OWN * BLK), OWN * BLK)], SL[:, cb * BLK : (cb + 1) * BLK],
            preferred_element_type=F32,
        )

    def g1(cb, to):
        return remote(GS1.at[cb], GR1.at[cb], g1s.at[cb], g1r.at[cb], to)

    def g2(way, cb, to):
        return remote(GS2.at[way, cb], GR2.at[way, cb], g2s.at[way, cb], g2r.at[way, cb], to)

    GS1[0] = grads(0, m2).astype(BF16)
    go(g1(0, to_up))
    GS1[1] = grads(1, m2).astype(BF16)
    go(g1(1, to_down))

    GS2[0, 1] = grads(1, m1).astype(BF16)
    go(g2(0, 1, to_up))
    GS2[1, 0] = grads(0, m3).astype(BF16)
    go(g2(1, 0, to_down))
    SLT[...] = SL[...].T

    def pair_copy(j, p):
        return remote(D.at[xa[j], side[p], :, oc], S.at[j, p], ss.at[j, p], sr.at[j, p], to_c)

    def terms(j, p):
        first = xa[j] * (RB // NX) + side[p] * (RB // NX // NY)

        def step(g, carry):
            picks = [(INV[0, first + g * 3 + n], INV[1, first + g * 3 + n]) for n in range(3)]
            halves = [jnp.concatenate([W[cb, k[cb]] for k in picks], axis=0) for cb in range(CB)]
            made = jnp.dot(jnp.concatenate(halves, axis=1), SLT[...], preferred_element_type=F32)
            D[xa[j], side[p], pl.ds(g * ZB, ZB)] = made.reshape(ZB, NC, SH, BLK).astype(BF16)
            return carry

        lax.fori_loop(0, NZ // ZB, step, 0)
        go(pair_copy(j, p))

    def both_cores(j, p, n):
        zz = za[RANK[n]]
        return D[xa[j], side[p], zz, c].astype(F32) + S[j, p, zz].astype(F32)

    def x_copy(j, p, i):
        at = pl.ds(*GROUPS[i])
        return remote(
            XS.at[j - 1, p, at], XR.at[j - 1, p, at], rxs.at[j - 1, p, i], rxr.at[j - 1, p, i], to_x[j]
        )

    def y_copy(i):
        at = pl.ds(*GROUPS[i])
        return remote(YS.at[at], YR.at[at], rys.at[i], ryr.at[i], to_y)

    def z_copy(n, to):
        back = RANK.index((NZ - RANK[n]) % NZ)
        return remote(ZS.at[n], ZR.at[back], rzs.at[n], rzr.at[back], to)

    def second(way, cb, to):
        g1(cb, to).wait_recv()
        GS2[way, cb] = (GP[cb] + GR1[cb].astype(F32)).astype(BF16)
        go(g2(way, cb, to))

    far_groups = range(NG - 1, -1, -1)

    def along_x(p, i):
        for j in FAR_FIRST:
            for n in ranks(i):
                XS[j - 1, p, n] = both_cores(j, p, n).astype(BF16)
            go(x_copy(j, p, i))

    for p in (1, 0):
        for j in (2, 1, 3, 0):
            terms(j, p)
    for p in (1, 0):
        for j in FAR_FIRST:
            pair_copy(j, p).wait_recv()
        for i in far_groups:
            if p == 1:
                along_x(1, i)
    for i in far_groups:
        along_x(0, i)
    for p in (1, 0):
        pair_copy(0, p).wait_recv()
        for n in range(NZ):
            OX[p, n] = both_cores(0, p, n)
    GP[0] = grads(0, m1)
    GP[1] = grads(1, m3)
    for cb in range(CB):
        bg_ref[cb] = grads(cb, m).reshape(OWN, BLK, BLK)

    def from_x(p, i):
        at = pl.ds(*GROUPS[i])
        total = OX[p, at]
        for j in FAR_FIRST:
            x_copy(j, p, i).wait_recv()
            total = total + XR[j - 1, p, at].astype(F32)
        return total

    for i in far_groups:
        YS[pl.ds(*GROUPS[i])] = from_x(1, i).astype(BF16)
        go(y_copy(i))
    for i in far_groups:
        at = pl.ds(*GROUPS[i])
        total = from_x(0, i)
        y_copy(i).wait_recv()
        total = total + YR[at].astype(F32)
        if i == 0:
            ZR0[...] = total
            continue
        ZS[at] = total.astype(BF16)
        for n in ranks(i):
            go(z_copy(n, to_z[RANK[n]]))
        if i == NG - 1:
            second(0, 0, to_up)
            second(1, 1, to_down)
    dx = ZR0[0]

    def add(way, cb):
        g2(way, cb, to_up).wait_recv()
        bg_ref[cb] = bg_ref[cb] + GR2[way, cb].astype(F32).reshape(OWN, BLK, BLK)

    for n in range(1, NZ):
        z_copy(RANK.index((NZ - RANK[n]) % NZ), to_y).wait_recv()
        dx = dx + ZR[n].astype(F32)
    dx_ref[...] = dx.astype(BF16)
    add(0, 1)
    add(1, 0)
    add(0, 0)
    add(1, 1)
    drain()


def body(activations, block_values, block_rows, cotangent):
    tokens = activations.shape[0]
    hbm, vmem = pl.BlockSpec(memory_space=pltpu.HBM), pl.BlockSpec(memory_space=pltpu.VMEM)
    dma = pltpu.SemaphoreType.DMA
    column = (OWN * BLK, BLK)
    gelu_out, dx, block_grad = pl.pallas_call(
        kernel,
        name="sparse_up_both_ways",
        out_shape=(
            jax.ShapeDtypeStruct((tokens, CB * BLK), BF16),
            jax.ShapeDtypeStruct((SH, tokens), BF16),
            jax.ShapeDtypeStruct((CB, OWN, BLK, BLK), F32),
        ),
        in_specs=[hbm] * 4,
        out_specs=(vmem, vmem, vmem),
        scratch_shapes=[
            pltpu.VMEM((NX, NY, NZ, NC, SH, BLK), BF16),
            pltpu.VMEM((CB, KB + 1, BLK, BLK), BF16),
            pltpu.VMEM((BLK, CB * BLK), BF16),
            pltpu.VMEM((NX, NY, NZ, NC, SH, BLK), BF16),
            pltpu.VMEM((RB, BLK, BLK), BF16),
            pltpu.VMEM((CB, KB * BLK, BLK), BF16),
            pltpu.VMEM((BLK, CB * BLK), BF16),
            pltpu.VMEM((CB * BLK, BLK), BF16),
            pltpu.VMEM((NX, NY, NZ, NC, SH, BLK), BF16),
            pltpu.VMEM((NX, NY, NZ, SH, BLK), BF16),
            pltpu.VMEM((NX - 1, NY, NZ, SH, BLK), BF16),
            pltpu.VMEM((NX - 1, NY, NZ, SH, BLK), BF16),
            pltpu.VMEM((NY, NZ, SH, BLK), F32),
            pltpu.VMEM((NZ, SH, BLK), BF16),
            pltpu.VMEM((NZ, SH, BLK), BF16),
            pltpu.VMEM((1, SH, BLK), F32),
            pltpu.VMEM((NZ, SH, BLK), BF16),
            pltpu.VMEM((NZ, SH, BLK), BF16),
            pltpu.VMEM((2, *column), BF16),
            pltpu.VMEM((2, *column), BF16),
            pltpu.VMEM((2, CB, *column), BF16),
            pltpu.VMEM((2, CB, *column), BF16),
            pltpu.VMEM((2, *column), F32),
            pltpu.VMEM((CB, BLK), jnp.int32),
            pltpu.SMEM((CB, KB), jnp.int32),
            pltpu.SMEM((CB, BLK), jnp.int32),
            dma((4,)),
            dma((NZ,)), dma((NZ,)),
            dma((NX, NG)), dma((NX, NG)),
            dma((NX - 1, NY, NG)), dma((NX - 1, NY, NG)),
            dma((NX, NY, NG)), dma((NX, NY, NG)),
            dma((NX, NY)), dma((NX, NY)),
            dma((NX - 1, NY, NG)), dma((NX - 1, NY, NG)),
            dma((NG,)), dma((NG,)),
            dma((NZ,)), dma((NZ,)),
            dma((2,)), dma((2,)),
            dma((2, CB)), dma((2, CB)),
        ],
        compiler_params=pltpu.CompilerParams(
            collective_id=0, has_side_effects=True, vmem_limit_bytes=52 << 20
        ),
    )(block_rows, activations.T, cotangent, block_values)
    return gelu_out, dx.T, block_grad


def solution(mesh):
    in_specs = (P("mp", "dp"), P("dp", None, None, None), P("dp", None), P("mp", "dp"))
    out_specs = (P("mp", "dp"), P("mp", "dp"), P("dp", "mp", None, None))
    return jax.shard_map(body, mesh=mesh, in_specs=in_specs, out_specs=out_specs, check_vma=False)
```

```python
import functools

import jax
import jax.numpy as jnp
from jax import lax
from jax.experimental import pallas as pl
from jax.experimental.pallas import tpu as pltpu
from jax.sharding import PartitionSpec as P

NX, NY, NZ, NC, NM = 4, 2, 12, 2, 4
BLK, KB, RB, CB = 128, 20, 72, 2
SH = 48
ZB = 4
RANK = (0, 1, 11, 2, 10, 3, 9, 4, 8, 5, 7, 6)
GROUPS = ((0, 1), (1, 2), (3, 4), (7, 5))
NG = len(GROUPS)
SUM_GROUPS = ((0, 1), (1, 6), (7, 5))
NS = len(SUM_GROUPS)
OWN = KB // NM
FAR_FIRST = (2, 1, 3)
F32, BF16 = jnp.float32, jnp.bfloat16
C0 = 0.7978845608028654
C1 = 0.044715


def coords():
    d = lax.axis_index("dp")
    c = lax.rem(d, NC)
    z = lax.rem(lax.div(d, NC), NZ)
    y = lax.rem(lax.div(d, NC * NZ), NY)
    x = lax.div(d, NC * NZ * NY)
    return x, y, z, c, lax.axis_index("mp")


def device(x, y, z, c, m):
    return (((x * NY + y) * NZ + z) * NC + c, m)


def remote(src, dst, send, recv, to):
    return pltpu.make_async_remote_copy(
        src_ref=src, dst_ref=dst, send_sem=send, recv_sem=recv,
        device_id=to, device_id_type=pl.DeviceIdType.MESH,
    )


def kernel(
    rows_hbm, xt_hbm, cot_hbm, w_hbm,
    gelu_ref, dx_ref, bg_ref,
    X, W, COT, XQ, XF, XP, SL, SLT, D, S, XS, XR, OX, YS, YR, ZR0, ZS, ZR,
    GS1, GR1, GS2, GR2, GP, IV, ROWS, INV,
    isem, zs, zr, ys, yr, xs, xr, bs, br,
    ss, sr, rxs, rxr, rys, ryr, rzs, rzr, g1s, g1r, g2s, g2r,
):
    x, y, z, c, m = coords()
    oy, oc = 1 - y, 1 - c
    side = (y, oy)
    xa = [x] + [lax.rem(x + j, NX) for j in range(1, NX)]
    za = [z] + [lax.rem(z + k, NZ) for k in range(1, NZ)]
    m1, m2, m3 = (lax.rem(m + k, NM) for k in (1, 2, 3))
    to_x = [None] + [device(xa[j], y, z, c, m) for j in range(1, NX)]
    to_z = [None] + [device(x, y, za[k], c, m) for k in range(1, NZ)]
    to_y = device(x, oy, z, c, m)
    to_c = device(x, y, z, oc, m)
    to_up, to_down = device(x, y, z, c, m1), device(x, y, z, c, m3)

    own_x = pltpu.make_async_copy(xt_hbm, X.at[0, 0, 0, 0], isem.at[0])
    rows_in = pltpu.make_async_copy(rows_hbm, ROWS, isem.at[1])
    w_in = pltpu.make_async_copy(w_hbm, W.at[:, pl.ds(0, KB)], isem.at[2])
    cot_in = pltpu.make_async_copy(cot_hbm, COT, isem.at[3])
    for copy in (own_x, rows_in, w_in, cot_in):
        copy.start()

    barrier = pltpu.get_barrier_semaphore()
    partners = to_z[1:] + to_x[1:] + [to_y, to_c, to_up, to_down]
    for d in partners:
        pl.semaphore_signal(barrier, inc=1, device_id=d, device_id_type=pl.DeviceIdType.MESH)
    own_x.wait()
    pl.semaphore_wait(barrier, len(partners))

    started = []

    def go(copy):
        copy.start()
        started.append(copy)

    def drain():
        for copy in started:
            copy.wait_send()
        started.clear()

    def ranks(i):
        return range(GROUPS[i][0], sum(GROUPS[i]))

    def part(j, p, i, cc=0):
        return X.at[j, p, pl.ds(*GROUPS[i]), cc]

    def z_in(n, to):
        back = RANK.index((NZ - RANK[n]) % NZ)
        return remote(X.at[0, 0, 0, 0], X.at[0, 0, back, 0], zs.at[back], zr.at[back], to)

    def x_in(j, p, i):
        return remote(part(0, p, i), part(j, p, i), xs.at[j - 1, p, i], xr.at[j - 1, p, i], to_x[j])

    def y_in(j, i):
        return remote(part(j, 0, i), part(j, 1, i), ys.at[j, i], yr.at[j, i], to_y)

    def c_in(j, p, i):
        return remote(part(j, p, i), part(j, p, i, 1), bs.at[j, p, i], br.at[j, p, i], to_c)

    def send_x(p, i):
        for j in FAR_FIRST:
            go(x_in(j, p, i))

    def y_then_x(i):
        y_in(0, i).wait_recv()
        send_x(1, i)
        go(c_in(0, 1, i))

    def x_then_y(i):
        for j in (1, 3, 2):
            x_in(j, 0, i).wait_recv()
            go(y_in(j, i))
            go(c_in(j, 0, i))

    for n in range(1, NZ):
        go(z_in(n, to_z[RANK[n]]))
    def along_z(i):
        for n in ranks(i):
            if n:
                z_in(RANK.index((NZ - RANK[n]) % NZ), to_y).wait_recv()
        go(y_in(0, i))
        send_x(0, i)
        go(c_in(0, 0, i))

    def x_to_core(p, i):
        for j in (1, 3, 2):
            x_in(j, p, i).wait_recv()
            go(c_in(j, p, i))

    along_z(0)
    along_z(1)
    y_then_x(0)
    along_z(2)
    y_then_x(1)
    x_to_core(0, 0)
    x_to_core(1, 0)
    x_to_core(0, 1)
    along_z(3)
    x_then_y(2)
    y_then_x(3)
    x_to_core(1, 1)

    rows_in.wait()
    lanes = lax.broadcasted_iota(jnp.int32, (1, BLK), 1)
    for cb in range(CB):
        found = jnp.full((1, BLK), KB, jnp.int32)
        for k in range(KB):
            found = jnp.where(lanes == ROWS[cb, k], k, found)
        IV[pl.ds(cb, 1)] = found
    inv_in = pltpu.make_async_copy(IV, INV, isem.at[1])
    inv_in.start()
    w_in.wait()
    cot_in.wait()
    for cb in range(CB):
        W[cb, KB] = jnp.zeros((BLK, BLK), BF16)
    inv_in.wait()

    for j in (0, 1, 3, 2):
        y_in(j, 2).wait_recv()
        go(c_in(j, 1, 2))
    x_to_core(0, 3)
    x_to_core(1, 3)
    for i in range(NG):
        for j in (0, 1, 3, 2):
            for p in range(NY):
                c_in(j, p, i).wait_recv()

    for j in range(NX):
        for p in range(NY):
            for n in range(NZ):
                XQ[xa[(NX - j) % NX], side[p], za[RANK[n]], c] = X[j, p, n, 0]
                XQ[xa[(NX - j) % NX], side[p], za[RANK[n]], oc] = X[j, p, n, 1]
    XF[...] = XQ[...].reshape(RB, BLK, BLK)
    for cb in range(CB):
        for k in range(KB):
            XP[cb, pl.ds(k * BLK, BLK)] = XF[ROWS[cb, k]]
    for cb in range(CB):
        cols = pl.ds(cb * BLK, BLK)
        v = lax.dot_general(
            XP[cb], W[cb, :KB].reshape(KB * BLK, BLK), (((0,), (0,)), ((), ())),
            preferred_element_type=F32,
        )
        t = jnp.tanh(C0 * (v + C1 * (v * v * v)))
        gelu_ref[:, cols] = (0.5 * v * (1.0 + t)).astype(BF16)
        slope = 0.5 * (1.0 + t) + 0.5 * v * (1.0 - t * t) * (C0 * (1.0 + 3.0 * C1 * (v * v)))
        SL[:, cols] = (COT[:, cols].astype(F32) * slope).astype(BF16)

    def grads(cb, group):
        return jnp.dot(
            XP[cb, pl.ds(group * (OWN * BLK), OWN * BLK)], SL[:, cb * BLK : (cb + 1) * BLK],
            preferred_element_type=F32,
        )

    def g1(cb, to):
        return remote(GS1.at[cb], GR1.at[cb], g1s.at[cb], g1r.at[cb], to)

    def g2(way, cb, to):
        return remote(GS2.at[way, cb], GR2.at[way, cb], g2s.at[way, cb], g2r.at[way, cb], to)

    GS1[0] = grads(0, m2).astype(BF16)
    go(g1(0, to_up))
    GS1[1] = grads(1, m2).astype(BF16)
    go(g1(1, to_down))

    GS2[0, 1] = grads(1, m1).astype(BF16)
    go(g2(0, 1, to_up))
    GS2[1, 0] = grads(0, m3).astype(BF16)
    go(g2(1, 0, to_down))
    SLT[...] = SL[...].T

    def pair_copy(j, p):
        return remote(D.at[xa[j], side[p], :, oc], S.at[j, p], ss.at[j, p], sr.at[j, p], to_c)

    def terms(j, p):
        first = xa[j] * (RB // NX) + side[p] * (RB // NX // NY)

        def step(g, carry):
            picks = [(INV[0, first + g * 3 + n], INV[1, first + g * 3 + n]) for n in range(3)]
            halves = [jnp.concatenate([W[cb, k[cb]] for k in picks], axis=0) for cb in range(CB)]
            made = jnp.dot(jnp.concatenate(halves, axis=1), SLT[...], preferred_element_type=F32)
            D[xa[j], side[p], pl.ds(g * ZB, ZB)] = made.reshape(ZB, NC, SH, BLK).astype(BF16)
            return carry

        lax.fori_loop(0, NZ // ZB, step, 0)
        go(pair_copy(j, p))

    def sum_ranks(i):
        return range(SUM_GROUPS[i][0], sum(SUM_GROUPS[i]))

    def both_cores(j, p, n):
        zz = za[RANK[n]]
        return D[xa[j], side[p], zz, c].astype(F32) + S[j, p, zz].astype(F32)

    def x_copy(j, p, i):
        at = pl.ds(*SUM_GROUPS[i])
        return remote(
            XS.at[j - 1, p, at], XR.at[j - 1, p, at], rxs.at[j - 1, p, i], rxr.at[j - 1, p, i], to_x[j]
        )

    def y_copy(i):
        at = pl.ds(*SUM_GROUPS[i])
        return remote(YS.at[at], YR.at[at], rys.at[i], ryr.at[i], to_y)

    def z_copy(n, to):
        back = RANK.index((NZ - RANK[n]) % NZ)
        return remote(ZS.at[n], ZR.at[back], rzs.at[n], rzr.at[back], to)

    def second(way, cb, to):
        g1(cb, to).wait_recv()
        GS2[way, cb] = (GP[cb] + GR1[cb].astype(F32)).astype(BF16)
        go(g2(way, cb, to))

    far_groups = range(NS - 1, -1, -1)

    def along_x(p, i):
        for j in FAR_FIRST:
            for n in sum_ranks(i):
                XS[j - 1, p, n] = both_cores(j, p, n).astype(BF16)
            go(x_copy(j, p, i))

    for p in (1, 0):
        for j in (2, 1, 3, 0):
            terms(j, p)
    for p in (1, 0):
        for j in FAR_FIRST:
            pair_copy(j, p).wait_recv()
        for i in far_groups:
            if p == 1:
                along_x(1, i)
    for i in far_groups:
        along_x(0, i)
    for p in (1, 0):
        pair_copy(0, p).wait_recv()
        for n in range(NZ):
            OX[p, n] = both_cores(0, p, n)
    GP[0] = grads(0, m1)
    GP[1] = grads(1, m3)
    for cb in range(CB):
        bg_ref[cb] = grads(cb, m).reshape(OWN, BLK, BLK)

    def from_x(p, i):
        at = pl.ds(*SUM_GROUPS[i])
        total = OX[p, at]
        for j in FAR_FIRST:
            x_copy(j, p, i).wait_recv()
            total = total + XR[j - 1, p, at].astype(F32)
        return total

    for i in far_groups:
        YS[pl.ds(*SUM_GROUPS[i])] = from_x(1, i).astype(BF16)
        go(y_copy(i))
    for i in far_groups:
        at = pl.ds(*SUM_GROUPS[i])
        total = from_x(0, i)
        y_copy(i).wait_recv()
        total = total + YR[at].astype(F32)
        if i == 0:
            ZR0[...] = total
            continue
        ZS[at] = total.astype(BF16)
        for n in sum_ranks(i):
            go(z_copy(n, to_z[RANK[n]]))
        if i == NS - 1:
            second(0, 0, to_up)
            second(1, 1, to_down)
    dx = ZR0[0]

    def add(way, cb):
        g2(way, cb, to_up).wait_recv()
        bg_ref[cb] = bg_ref[cb] + GR2[way, cb].astype(F32).reshape(OWN, BLK, BLK)

    for n in range(1, NZ):
        z_copy(RANK.index((NZ - RANK[n]) % NZ), to_y).wait_recv()
        dx = dx + ZR[n].astype(F32)
    dx_ref[...] = dx.astype(BF16)
    add(0, 1)
    add(1, 0)
    add(0, 0)
    add(1, 1)
    drain()


def body(activations, block_values, block_rows, cotangent):
    tokens = activations.shape[0]
    hbm, vmem = pl.BlockSpec(memory_space=pltpu.HBM), pl.BlockSpec(memory_space=pltpu.VMEM)
    dma = pltpu.SemaphoreType.DMA
    column = (OWN * BLK, BLK)
    gelu_out, dx, block_grad = pl.pallas_call(
        kernel,
        name="sparse_up_both_ways",
        out_shape=(
            jax.ShapeDtypeStruct((tokens, CB * BLK), BF16),
            jax.ShapeDtypeStruct((SH, tokens), BF16),
            jax.ShapeDtypeStruct((CB, OWN, BLK, BLK), F32),
        ),
        in_specs=[hbm] * 4,
        out_specs=(vmem, vmem, vmem),
        scratch_shapes=[
            pltpu.VMEM((NX, NY, NZ, NC, SH, BLK), BF16),
            pltpu.VMEM((CB, KB + 1, BLK, BLK), BF16),
            pltpu.VMEM((BLK, CB * BLK), BF16),
            pltpu.VMEM((NX, NY, NZ, NC, SH, BLK), BF16),
            pltpu.VMEM((RB, BLK, BLK), BF16),
            pltpu.VMEM((CB, KB * BLK, BLK), BF16),
            pltpu.VMEM((BLK, CB * BLK), BF16),
            pltpu.VMEM((CB * BLK, BLK), BF16),
            pltpu.VMEM((NX, NY, NZ, NC, SH, BLK), BF16),
            pltpu.VMEM((NX, NY, NZ, SH, BLK), BF16),
            pltpu.VMEM((NX - 1, NY, NZ, SH, BLK), BF16),
            pltpu.VMEM((NX - 1, NY, NZ, SH, BLK), BF16),
            pltpu.VMEM((NY, NZ, SH, BLK), F32),
            pltpu.VMEM((NZ, SH, BLK), BF16),
            pltpu.VMEM((NZ, SH, BLK), BF16),
            pltpu.VMEM((1, SH, BLK), F32),
            pltpu.VMEM((NZ, SH, BLK), BF16),
            pltpu.VMEM((NZ, SH, BLK), BF16),
            pltpu.VMEM((2, *column), BF16),
            pltpu.VMEM((2, *column), BF16),
            pltpu.VMEM((2, CB, *column), BF16),
            pltpu.VMEM((2, CB, *column), BF16),
            pltpu.VMEM((2, *column), F32),
            pltpu.VMEM((CB, BLK), jnp.int32),
            pltpu.SMEM((CB, KB), jnp.int32),
            pltpu.SMEM((CB, BLK), jnp.int32),
            dma((4,)),
            dma((NZ,)), dma((NZ,)),
            dma((NX, NG)), dma((NX, NG)),
            dma((NX - 1, NY, NG)), dma((NX - 1, NY, NG)),
            dma((NX, NY, NG)), dma((NX, NY, NG)),
            dma((NX, NY)), dma((NX, NY)),
            dma((NX - 1, NY, NS)), dma((NX - 1, NY, NS)),
            dma((NS,)), dma((NS,)),
            dma((NZ,)), dma((NZ,)),
            dma((2,)), dma((2,)),
            dma((2, CB)), dma((2, CB)),
        ],
        compiler_params=pltpu.CompilerParams(
            collective_id=0, has_side_effects=True, vmem_limit_bytes=52 << 20
        ),
    )(block_rows, activations.T, cotangent, block_values)
    return gelu_out, dx.T, block_grad


def solution(mesh):
    in_specs = (P("mp", "dp"), P("dp", None, None, None), P("dp", None), P("mp", "dp"))
    out_specs = (P("mp", "dp"), P("mp", "dp"), P("dp", "mp", None, None))
    return jax.shard_map(body, mesh=mesh, in_specs=in_specs, out_specs=out_specs, check_vma=False)
```
